128 devices in a mesh: seq: 8 (over y, x_hi), chan: 16 (over x_lo, z, core).
Axes of the slice: x: 4 (x_hi: 2, x_lo: 2; x = x_hi * 2 + x_lo), y: 4, z: 4, core: 2. Of those that a mesh axis runs over, the one named last changes fastest.
Arguments:
- query_rows: bfloat16 [8192, 8192], P('seq', 'chan'), may hold values from -6 to 6
- key_rows: bfloat16 [8192, 8192], P('seq', 'chan'), may hold values from -6 to 6
- value_rows: bfloat16 [8192, 8192], P('seq', 'chan'), may hold values from -6 to 6
- horizon: float32 [16, 8192], P(None, 'chan'), may hold values from 30 to 32768
- residue: float32 [16, 8192], P(None, 'chan'), may hold values from -1.5 to 1.5
- skip: float32 [8192], P('chan'), may hold values from -4 to 4
- w_out: bfloat16 [8192, 8192], P('chan'), may hold values from -0.09375 to 0.09375
Outputs:
- output: bfloat16 [8192, 8192], P('seq', 'chan')
The draws below stay inside these ranges and needn't reach their ends.
All inputs are finite; a program needn't handle non-finite values.
Results may differ from the reference program's by a relative error of at most 0.0049.
Values may be sent and summed in bfloat16 or wider, within the bound.
A program may use at most 192 MiB of HBM per device.

```python
import math
import jax
import jax.numpy as jnp
from jax import lax

D = 8192
M = 16
TOKENS = 8192


def draw_horizon(key, part):
    chooser, slow_key, fast_key = jax.random.split(key, 3)
    whole = float(TOKENS)
    slow_lower = math.log(whole / 2.0)
    slow_upper = math.log(4.0 * whole)
    fast_lower = math.log(30.0)
    fast_upper = math.log(max(whole / 2.0, 31.0))
    share = 0.5
    slow_vals = jnp.exp(jax.random.uniform(slow_key, (M, D), jnp.float32, slow_lower, slow_upper))
    fast_vals = jnp.exp(jax.random.uniform(fast_key, (M, D), jnp.float32, fast_lower, fast_upper))
    picked = jax.random.uniform(chooser, (M, D), jnp.float32) < share
    return jnp.clip(jnp.where(picked, slow_vals, fast_vals), 30.0, 4.0 * whole)


def spiked(result, rng, source, target, blocks, factor):
    def block_of(dim):
        return (jnp.arange(result.shape[dim]) // (result.shape[dim] // blocks)).reshape((-1,) + (1,) * (result.ndim - 1 - dim))

    one_side = jax.random.permutation(rng, blocks)[block_of(target)]
    other_side = (block_of(target) + blocks // 2) % blocks
    return jnp.where((block_of(source) == one_side) | (block_of(source) == other_side), factor * result, result)


def level_of(rng, shape, cuts, least, top_value):
    def one(axis_at, blocks):
        heights = jax.random.uniform(jax.random.fold_in(jax.random.fold_in(rng, 6), axis_at), (blocks,), jnp.float32, least / len(cuts), top_value / len(cuts))
        return jnp.repeat(jnp.exp(heights), shape[axis_at] // blocks).reshape((-1,) + (1,) * (len(shape) - axis_at - 1))

    gain = one(*cuts[0])
    for cut in cuts[1:]:
        gain = gain * one(*cut)
    return gain


def normal_values(key, dims, scale, most, cuts=(), kind=jnp.bfloat16):
    drawn = jax.random.normal(key, dims, jnp.float32) * scale
    if len(cuts) > 0:
        drawn = level_of(key, dims, cuts, -0.22, 0.18) * drawn
    return jnp.clip(drawn, min=-most, max=most).astype(kind)


def gaussian_with(rng, extent, scale, limit, cuts, heavy, kind=jnp.bfloat16):
    array = scale * jax.random.normal(rng, extent, jnp.float32)
    if cuts:
        array = array * level_of(rng, extent, cuts, -0.22, 0.18)
    return jnp.clip(spiked(array, jax.random.fold_in(rng, 3), *heavy), -limit, limit).astype(kind)


def setup_inputs(seed: int = 0) -> dict:
    streams_of = jax.random.split(jax.random.key(seed), 8)
    return {
        "query_rows": normal_values(streams_of[0], (TOKENS, D), 1.0, 6.0, ((0, 8), (1, 16))),
        "key_rows": normal_values(streams_of[1], (TOKENS, D), 1.0, 6.0, ((0, 8), (1, 16))),
        "value_rows": normal_values(streams_of[2], (TOKENS, D), 1.0, 6.0, ((0, 8), (1, 16))),
        "horizon": draw_horizon(jax.random.fold_in(streams_of[7], 71), 0),
        "residue": normal_values(streams_of[4], (M, D), M ** -0.5, 1.5, ((1, 16),), jnp.float32),
        "skip": normal_values(streams_of[5], (D,), 1.0, 4.0, ((0, 16),), jnp.float32),
        "w_out": gaussian_with(streams_of[6], (D, D), D ** -0.5, 0.09375, ((0, 16),), (0, 1, 16, 2.0)),
    }


def reference(query_rows, key_rows, value_rows, horizon, residue, skip, w_out):
    total_rows, width = query_rows.shape
    block_len = min(128, total_rows)
    block_count = total_rows // block_len
    rate = 1.0 / horizon
    scaled = residue * jnp.sqrt(-jnp.expm1(-2.0 * rate))
    mixed = key_rows.astype(jnp.float32) * value_rows.astype(jnp.float32)
    pieces = mixed.reshape(block_count, block_len, width)
    step_index = jnp.arange(block_len, dtype=jnp.int32)
    offsets = step_index.astype(jnp.float32)
    powers = jnp.exp(-rate[:, None, :] * offsets[None, :, None])
    kernel = lax.optimization_barrier(jnp.sum(powers * scaled[:, None, :], axis=0))
    lags = step_index[:, None] - step_index[None, :]
    toeplitz = jnp.where((lags >= 0)[:, :, None], jnp.take(kernel, jnp.maximum(lags, 0), axis=0), 0.0)
    lead = powers * (scaled * jnp.exp(-rate))[:, None, :]
    tail = powers[:, ::-1, :]
    block_decay = jnp.exp(-rate * block_len)

    def advance(state, piece):
        inner = jnp.einsum('tsc,sc->tc', toeplitz, piece, precision=lax.Precision.HIGHEST)
        outer = jnp.einsum('mtc,mc->tc', lead, state, precision=lax.Precision.HIGHEST)
        local_end = jnp.einsum('msc,sc->mc', tail, piece, precision=lax.Precision.HIGHEST)
        return (block_decay * state + local_end, inner + outer)
    start_state = jnp.zeros(horizon.shape, jnp.float32)
    _, conv_blocks = lax.scan(advance, start_state, pieces)
    conv = conv_blocks.reshape(total_rows, width)
    gated = (query_rows.astype(jnp.float32) * (conv + skip[None, :] * mixed)).astype(jnp.bfloat16)
    return jnp.dot(gated, w_out, preferred_element_type=jnp.float32).astype(jnp.bfloat16)
```

```python
import functools

import jax
import jax.numpy as jnp
from jax import lax
from jax.experimental import pallas as pl
from jax.experimental.pallas import tpu as pltpu
from jax.sharding import PartitionSpec as P

MESH = pl.DeviceIdType.MESH
F32 = jnp.float32
BF16 = jnp.bfloat16

ROWS = 1024
WIDTH = 512
MODES = 16
SUB = 8
BLOCK = ROWS // SUB
LANES = 128
TILES = WIDTH // LANES
CHUNKS = 8
CHUNK = ROWS // CHUNKS
LAG2 = 2
LAG3 = 4
VIA = {2: (0, 1), 1: (0, 1), 3: (0, 1), 0: (1, 1)}
ORDER = (2, 1, 3, 0)


def place(y, xh, xl, z, core):
    return {"seq": y * 2 + xh, "chan": xl * 8 + z * 2 + core}


def kernel(
    q_hbm, k_hbm, v_hbm, horizon_ref, residue_ref, skip_ref, w_hbm, out_ref,
    stage, mix, gate, decay, coef, skips, local, begin, ends, gat, wn,
    first_out, first_in, second_out, second_in, total,
    stage_sem, wl, wc_s, wc_r, wx_s, wx_r, wy_s, wy_r, st_s, st_r,
    gc_s, gc_r, gx_s, gx_r, gf_s, gf_r, f_s, f_r, s_s, s_r,
):
    seq = lax.axis_index("seq")
    chan = lax.axis_index("chan")
    y, xh = seq // 2, lax.rem(seq, 2)
    xl, z, core = chan // 8, lax.rem(chan // 2, 4), lax.rem(chan, 2)
    parity = lax.rem(y, 2)

    def later(k):
        return {"seq": lax.rem(seq + k, 8), "chan": chan}

    def x_side(hi, c):
        other = lax.rem(core + c, 2)
        return place(y, (1 - xh) if hi else xh, 1 - xl, z, other)

    mate = place(y, xh, xl, z, 1 - core)
    z_up = place(y, xh, xl, lax.rem(z + 1, 4), core)
    z_down = place(y, xh, xl, lax.rem(z + 3, 4), core)
    y_up = place(lax.rem(y + 1, 4), xh, xl, z, core)
    y_down = place(lax.rem(y + 3, 4), xh, xl, z, core)

    barrier = pltpu.get_barrier_semaphore()
    peers = [later(k) for k in range(1, 8)]
    peers += [mate, z_up, z_down]
    peers += [x_side(hi, c) for hi in (0, 1) for c in (0, 1)]
    for peer in peers:
        pl.semaphore_signal(barrier, inc=1, device_id=peer, device_id_type=MESH)

    loads = [
        pltpu.make_async_copy(src, stage.at[i], stage_sem.at[i])
        for i, src in enumerate((k_hbm, v_hbm, q_hbm))
    ]
    for load in loads:
        load.start()

    def remote(src, dst, send, recv, device):
        return pltpu.make_async_remote_copy(
            src_ref=src, dst_ref=dst, send_sem=send, recv_sem=recv,
            device_id=device, device_id_type=MESH,
        )

    def columns(a, d, b):
        block = a * 8 + lax.rem(z + d, 4) * 2 + b
        return pl.ds(pl.multiple_of(block * WIDTH, WIDTH), WIDTH)

    half = WIDTH // 2

    def half_rows(c, p):
        return pl.ds(pl.multiple_of((2 + c) * WIDTH + p * half, half), half)

    def w_x(d, c):
        return remote(
            w_hbm.at[pl.ds(pl.multiple_of(parity * half, half), half),
                     columns(1 - xl, d, lax.rem(core + c, 2))],
            wn.at[d, half_rows(c, parity)],
            wx_s.at[d, c], wx_r.at[d, c], x_side(VIA[d][c], c),
        )

    def w_y(d, c):
        piece = wn.at[d, half_rows(c, parity)]
        return remote(piece, piece, wy_s.at[d, c], wy_r.at[d, c], y_up if c else y_down)

    def w_mate(d):
        return remote(
            w_hbm.at[:, columns(xl, d, 1 - core)],
            wn.at[d, pl.ds(WIDTH, WIDTH)],
            wc_s.at[d], wc_r.at[d], mate,
        )

    def w_own(d):
        return pltpu.make_async_copy(
            w_hbm.at[:, columns(xl, d, core)], wn.at[d, pl.ds(0, WIDTH)], wl.at[d]
        )

    pl.semaphore_wait(barrier, len(peers))
    for d in ORDER:
        for c in (0, 1):
            w_x(d, c).start()
    for d in ORDER:
        w_mate(d).start()
    for d in ORDER:
        w_own(d).start()

    rate = 1.0 / horizon_ref[...]
    twice = 2.0 * rate
    series = jnp.ones_like(twice)
    for n in range(13, 1, -1):
        series = 1.0 - (twice * (1.0 / n)) * series
    power = jnp.where(twice < 0.5, twice * series, 1.0 - jnp.exp(-twice))
    scaled = residue_ref[...] * jnp.sqrt(power)
    step_decay = jnp.exp(-rate)
    block_decay = jnp.exp(-rate * BLOCK)
    device_decay = jnp.exp(-rate * ROWS)
    for t in range(TILES):
        lane = slice(t * LANES, (t + 1) * LANES)
        for m in range(MODES):
            rows = slice(m * SUB, (m + 1) * SUB)
            decay[t, rows, :] = jnp.broadcast_to(step_decay[m:m + 1, lane], (SUB, LANES))
            coef[t, rows, :] = jnp.broadcast_to(scaled[m:m + 1, lane], (SUB, LANES))
        skips[t, :, :] = jnp.broadcast_to(skip_ref[:, lane], (SUB, LANES))

    loads[0].wait()
    loads[1].wait()
    for t in range(TILES):
        lane = pl.ds(t * LANES, LANES)
        for n in range(SUB):
            rows = pl.ds(n * BLOCK, BLOCK)
            mix[t, pl.ds(n, BLOCK, stride=SUB), :] = (
                stage[0, rows, lane].astype(F32) * stage[1, rows, lane].astype(F32)
            )

    def states(ref, t):
        return [ref[t, m * SUB:(m + 1) * SUB, :] for m in range(MODES)]

    def scan_tile(t, carry):
        a = states(decay, t)

        def step(i, h):
            h = list(h)
            for u in range(4):
                x = mix[t, pl.ds(pl.multiple_of((i * 4 + u) * SUB, SUB), SUB), :]
                h = [a[m] * h[m] + x for m in range(MODES)]
            return tuple(h)

        zero = tuple(jnp.zeros((SUB, LANES), F32) for _ in range(MODES))
        h = lax.fori_loop(0, BLOCK // 4, step, zero)
        for m in range(MODES):
            local[t, m * SUB:(m + 1) * SUB, :] = h[m]
        return carry

    lax.fori_loop(0, TILES, scan_tile, 0)

    for t in range(TILES):
        lane = slice(t * LANES, (t + 1) * LANES)
        state = jnp.zeros((MODES, LANES), F32)
        for n in range(SUB):
            begin[t, pl.ds(n, MODES, stride=SUB), :] = state
            state = block_decay[:, lane] * state + local[t, pl.ds(n, MODES, stride=SUB), :]
        ends[0, :, lane] = state

    def state_copy(k):
        return remote(ends.at[0], ends.at[k], st_s.at[k], st_r.at[k], later(k))

    for k in range(1, 8):
        state_copy(k).start()

    loads[2].wait()
    for t in range(TILES):
        lane = pl.ds(t * LANES, LANES)
        for n in range(SUB):
            gate[t, pl.ds(n, BLOCK, stride=SUB), :] = (
                stage[2, pl.ds(n * BLOCK, BLOCK), lane].astype(F32)
            )

    def pass_on(d):
        for c in (0, 1):
            w_x(d, c).wait_recv()
            w_y(d, c).start()

    for k in range(1, 8):
        state_copy(k).wait_recv()
    incoming = jnp.zeros((MODES, WIDTH), F32)
    for k in range(7, 0, -1):
        incoming = jnp.where(k <= seq, device_decay * incoming + ends[k], incoming)
    for n in range(SUB):
        carried = jnp.exp(-rate * (BLOCK * n)) * incoming
        for t in range(TILES):
            rows = pl.ds(n, MODES, stride=SUB)
            begin[t, rows, :] = begin[t, rows, :] + carried[:, t * LANES:(t + 1) * LANES]

    def chunk_rows(r):
        return pl.ds(pl.multiple_of(r * CHUNK, CHUNK), CHUNK)

    def slot(s):
        return pl.ds(s * WIDTH, WIDTH)

    def g_mate(r):
        return remote(
            gat.at[chunk_rows(r), slot(0)], gat.at[chunk_rows(r), slot(1)],
            gc_s.at[r], gc_r.at[r], mate,
        )

    def g_x(r):
        return remote(
            gat.at[chunk_rows(r), slot(0)], gat.at[chunk_rows(r), slot(2)],
            gx_s.at[r], gx_r.at[r], x_side(0, 0),
        )

    def g_pass(r):
        return remote(
            gat.at[chunk_rows(r), slot(2)], gat.at[chunk_rows(r), slot(3)],
            gf_s.at[r], gf_r.at[r], mate,
        )

    def filter_tile(r, t):
        a = states(decay, t)
        b = states(coef, t)
        direct = skips[t, :, :]

        def step(i, h):
            h = list(h)
            parts = []
            base = r * CHUNK + i * (2 * SUB)
            for u in range(2):
                rows = pl.ds(pl.multiple_of(base + u * SUB, SUB), SUB)
                x = mix[t, rows, :]
                h = [a[m] * h[m] + x for m in range(MODES)]
                terms = [b[m] * h[m] for m in range(MODES)]
                while len(terms) > 1:
                    terms = [terms[j] + terms[j + 1] for j in range(0, len(terms), 2)]
                parts.append(gate[t, rows, :] * (terms[0] + direct * x))
            gat[
                pl.ds(pl.multiple_of(base, 2 * SUB), 2 * SUB),
                pl.ds(pl.multiple_of(t * LANES, LANES), LANES),
            ] = jnp.concatenate(parts, axis=0).astype(BF16)
            return tuple(h)

        h = lax.fori_loop(0, CHUNK // (2 * SUB), step, tuple(states(begin, t)))
        for m in range(MODES):
            begin[t, m * SUB:(m + 1) * SUB, :] = h[m]

    def filter_chunk(r, carry):
        def tile(t, carry):
            filter_tile(r, t)
            return carry

        lax.fori_loop(0, TILES, tile, 0)
        g_x(r).start()
        g_mate(r).start()
        return carry

    lax.fori_loop(0, CHUNKS, filter_chunk, 0)
    pass_on(2)
    pass_on(1)

    def w_ready(d):
        for c in (0, 1):
            w_y(d, c).wait_recv()
        w_mate(d).wait_recv()
        w_own(d).wait()

    def product(r, d):
        return jnp.dot(gat[chunk_rows(r), :], wn[d], preferred_element_type=F32)

    def first_copy(r, side):
        part = pl.ds(side * half, half)
        return remote(
            first_out.at[chunk_rows(r), part], first_in.at[chunk_rows(r), part],
            f_s.at[side, r], f_r.at[side, r], z_down if side else z_up,
        )

    def second_copy(r, side):
        return remote(
            second_out.at[side, chunk_rows(r)], second_in.at[side, chunk_rows(r)],
            s_s.at[side, r], s_r.at[side, r], z_down if side else z_up,
        )

    def first_sum(r):
        g_x(r).wait_recv()
        g_pass(r).start()
        g_mate(r).wait_recv()
        g_pass(r).wait_recv()
        first_out[chunk_rows(r), :] = product(r, 2).astype(BF16)
        for side in (0, 1):
            first_copy(r, side).start()

    def second_sum(r):
        for side in (0, 1):
            part = pl.ds(side * half, half)
            rest = pl.ds((1 - side) * half, half)
            partial = product(r, 3 if side else 1)
            first_copy(r, side).wait_recv()
            summed = partial[:, side * half:(side + 1) * half] + first_in[chunk_rows(r), part].astype(F32)
            second_out[side, chunk_rows(r), part] = summed.astype(BF16)
            second_out[side, chunk_rows(r), rest] = partial[:, (1 - side) * half:(2 - side) * half].astype(BF16)
            second_copy(r, side).start()

    def last_sum(r):
        own = product(r, 0)
        for side in (0, 1):
            second_copy(r, side).wait_recv()
        own = own + second_in[0, chunk_rows(r), :].astype(F32) + second_in[1, chunk_rows(r), :].astype(F32)
        for t in range(TILES):
            total[t, :, :] = own[:, t * LANES:(t + 1) * LANES]
        piece = CHUNK // SUB
        for n in range(SUB):
            rows = pl.ds(pl.multiple_of(n * BLOCK + r * piece, piece), piece)
            for t in range(TILES):
                out_ref[rows, t * LANES:(t + 1) * LANES] = (
                    total[t, pl.ds(n, piece, stride=SUB), :].astype(BF16)
                )

    def turn(i, carry):
        @pl.when(i == 0)
        def _():
            w_ready(2)

        @pl.when(i < CHUNKS)
        def _():
            first_sum(i)

        @pl.when(i == LAG2 - 1)
        def _():
            pass_on(3)

        @pl.when(i == LAG2)
        def _():
            w_ready(1)
            w_ready(3)

        @pl.when((i >= LAG2) & (i < CHUNKS + LAG2))
        def _():
            second_sum(i - LAG2)

        @pl.when(i == LAG3 - 1)
        def _():
            pass_on(0)

        @pl.when(i == LAG3)
        def _():
            w_ready(0)

        @pl.when(i >= LAG3)
        def _():
            last_sum(i - LAG3)

        return carry

    lax.fori_loop(0, CHUNKS + LAG3, turn, 0)

    for d in ORDER:
        for c in (0, 1):
            w_x(d, c).wait_send()
            w_y(d, c).wait_send()
        w_mate(d).wait_send()
    for k in range(1, 8):
        state_copy(k).wait_send()

    def finish(r, carry):
        g_x(r).wait_send()
        g_mate(r).wait_send()
        g_pass(r).wait_send()
        for side in (0, 1):
            first_copy(r, side).wait_send()
            second_copy(r, side).wait_send()
        return carry

    lax.fori_loop(0, CHUNKS, finish, 0)


def local(query_rows, key_rows, value_rows, horizon, residue, skip, w_out):
    dma = pltpu.SemaphoreType.DMA
    hbm = pl.BlockSpec(memory_space=pl.ANY)
    vmem = pl.BlockSpec(memory_space=pltpu.VMEM)
    return pl.pallas_call(
        kernel,
        out_shape=jax.ShapeDtypeStruct((ROWS, WIDTH), BF16),
        in_specs=[hbm, hbm, hbm, vmem, vmem, vmem, hbm],
        out_specs=vmem,
        scratch_shapes=[
            pltpu.VMEM((3, ROWS, WIDTH), BF16),
            pltpu.VMEM((TILES, ROWS, LANES), F32),
            pltpu.VMEM((TILES, ROWS, LANES), F32),
            pltpu.VMEM((TILES, MODES * SUB, LANES), F32),
            pltpu.VMEM((TILES, MODES * SUB, LANES), F32),
            pltpu.VMEM((TILES, SUB, LANES), F32),
            pltpu.VMEM((TILES, MODES * SUB, LANES), F32),
            pltpu.VMEM((TILES, MODES * SUB, LANES), F32),
            pltpu.VMEM((8, MODES, WIDTH), F32),
            pltpu.VMEM((ROWS, 4 * WIDTH), BF16),
            pltpu.VMEM((4, 4 * WIDTH, WIDTH), BF16),
            pltpu.VMEM((ROWS, WIDTH), BF16),
            pltpu.VMEM((ROWS, WIDTH), BF16),
            pltpu.VMEM((2, ROWS, WIDTH), BF16),
            pltpu.VMEM((2, ROWS, WIDTH), BF16),
            pltpu.VMEM((TILES, CHUNK, LANES), F32),
            dma((3,)), dma((4,)), dma((4,)), dma((4,)),
            dma((4, 2)), dma((4, 2)), dma((4, 2)), dma((4, 2)),
            dma((8,)), dma((8,)),
            dma((CHUNKS,)), dma((CHUNKS,)), dma((CHUNKS,)), dma((CHUNKS,)),
            dma((CHUNKS,)), dma((CHUNKS,)),
            dma((2, CHUNKS)), dma((2, CHUNKS)), dma((2, CHUNKS)), dma((2, CHUNKS)),
        ],
        compiler_params=pltpu.CompilerParams(
            collective_id=0, has_side_effects=True, vmem_limit_bytes=48 << 20
        ),
        cost_estimate=pl.CostEstimate(
            flops=2 * ROWS * 16 * WIDTH * WIDTH, bytes_accessed=13 << 20, transcendentals=0
        ),
        name="layer",
    )(query_rows, key_rows, value_rows, horizon, residue, skip.reshape(1, WIDTH), w_out)


def solution(mesh):
    in_specs = (
        P("seq", "chan"),
        P("seq", "chan"),
        P("seq", "chan"),
        P(None, "chan"),
        P(None, "chan"),
        P("chan"),
        P("chan", None),
    )
    out_specs = P("seq", "chan")
    return jax.shard_map(local, mesh=mesh, in_specs=in_specs, out_specs=out_specs, check_vma=False)
```

```python
import functools

import jax
import jax.numpy as jnp
from jax import lax
from jax.experimental import pallas as pl
from jax.experimental.pallas import tpu as pltpu
from jax.sharding import PartitionSpec as P

MESH = pl.DeviceIdType.MESH
F32 = jnp.float32
BF16 = jnp.bfloat16

ROWS = 1024
WIDTH = 512
MODES = 16
SUB = 8
BLOCK = ROWS // SUB
LANES = 128
TILES = WIDTH // LANES
CHUNKS = 8
CHUNK = ROWS // CHUNKS
LAG_UP = 2
LAG_DOWN = 5
LAG_LAST = 7
VIA = {2: (0, 1), 1: (0, 1), 3: (1, 1), 0: (0, 1)}
ORDER = (2, 1, 3, 0)


def place(y, xh, xl, z, core):
    return {"seq": y * 2 + xh, "chan": xl * 8 + z * 2 + core}


def kernel(
    q_hbm, k_hbm, v_hbm, horizon_hbm, residue_hbm, skip_hbm, w_hbm, out_ref,
    stage, horizon_ref, residue_ref, skip_ref, mix, gate, decay, coef, skips, local, begin, ends, gat, wn,
    first_out, first_in, second_out, second_in, total,
    stage_sem, small_sem, wl, wc_s, wc_r, wx_s, wx_r, wy_s, wy_r, st_s, st_r,
    gc_s, gc_r, gx_s, gx_r, gf_s, gf_r, f_s, f_r, s_s, s_r,
):
    seq = lax.axis_index("seq")
    chan = lax.axis_index("chan")
    y, xh = seq // 2, lax.rem(seq, 2)
    xl, z, core = chan // 8, lax.rem(chan // 2, 4), lax.rem(chan, 2)
    parity = lax.rem(y, 2)

    def later(k):
        return {"seq": lax.rem(seq + k, 8), "chan": chan}

    def x_side(hi, c):
        other = lax.rem(core + c, 2)
        return place(y, (1 - xh) if hi else xh, 1 - xl, z, other)

    mate = place(y, xh, xl, z, 1 - core)
    z_up = place(y, xh, xl, lax.rem(z + 1, 4), core)
    z_down = place(y, xh, xl, lax.rem(z + 3, 4), core)
    y_up = place(lax.rem(y + 1, 4), xh, xl, z, core)
    y_down = place(lax.rem(y + 3, 4), xh, xl, z, core)

    barrier = pltpu.get_barrier_semaphore()
    peers = [later(k) for k in range(1, 8)]
    peers += [mate, z_up, z_down]
    peers += [x_side(hi, c) for hi in (0, 1) for c in (0, 1)]
    for peer in peers:
        pl.semaphore_signal(barrier, inc=1, device_id=peer, device_id_type=MESH)

    loads = [
        pltpu.make_async_copy(src, stage.at[i], stage_sem.at[i])
        for i, src in enumerate((k_hbm, v_hbm, q_hbm))
    ]
    small = [
        pltpu.make_async_copy(src, dst, small_sem.at[i])
        for i, (src, dst) in enumerate(
            ((horizon_hbm, horizon_ref), (residue_hbm, residue_ref), (skip_hbm, skip_ref))
        )
    ]
    for load in small + loads:
        load.start()

    def remote(src, dst, send, recv, device):
        return pltpu.make_async_remote_copy(
            src_ref=src, dst_ref=dst, send_sem=send, recv_sem=recv,
            device_id=device, device_id_type=MESH,
        )

    def columns(a, d, b):
        block = a * 8 + lax.rem(z + d, 4) * 2 + b
        return pl.ds(pl.multiple_of(block * WIDTH, WIDTH), WIDTH)

    half = WIDTH // 2

    def half_rows(c, p):
        return pl.ds(pl.multiple_of((2 + c) * WIDTH + p * half, half), half)

    def w_x(d, c):
        return remote(
            w_hbm.at[pl.ds(pl.multiple_of(parity * half, half), half),
                     columns(1 - xl, d, lax.rem(core + c, 2))],
            wn.at[d, half_rows(c, parity)],
            wx_s.at[d, c], wx_r.at[d, c], x_side(VIA[d][c], c),
        )

    def w_y(d, c):
        piece = wn.at[d, half_rows(c, parity)]
        return remote(piece, piece, wy_s.at[d, c], wy_r.at[d, c], y_up if c else y_down)

    def w_mate(d):
        return remote(
            w_hbm.at[:, columns(xl, d, 1 - core)],
            wn.at[d, pl.ds(WIDTH, WIDTH)],
            wc_s.at[d], wc_r.at[d], mate,
        )

    def w_own(d):
        return pltpu.make_async_copy(
            w_hbm.at[:, columns(xl, d, core)], wn.at[d, pl.ds(0, WIDTH)], wl.at[d]
        )

    pl.semaphore_wait(barrier, len(peers))
    for c in (0, 1):
        w_x(2, c).start()
    for d in ORDER:
        w_mate(d).start()
    for d in ORDER:
        w_own(d).start()

    for load in small:
        load.wait()
    rate = 1.0 / horizon_ref[...]
    twice = 2.0 * rate
    series = jnp.ones_like(twice)
    for n in range(13, 1, -1):
        series = 1.0 - (twice * (1.0 / n)) * series
    power = jnp.where(twice < 0.5, twice * series, 1.0 - jnp.exp(-twice))
    scaled = residue_ref[...] * jnp.sqrt(power)
    step_decay = jnp.exp(-rate)
    block_decay = jnp.exp(-rate * BLOCK)
    device_decay = jnp.exp(-rate * ROWS)
    for t in range(TILES):
        lane = slice(t * LANES, (t + 1) * LANES)
        for m in range(MODES):
            rows = slice(m * SUB, (m + 1) * SUB)
            decay[t, rows, :] = jnp.broadcast_to(step_decay[m:m + 1, lane], (SUB, LANES))
            coef[t, rows, :] = jnp.broadcast_to(scaled[m:m + 1, lane], (SUB, LANES))
        skips[t, :, :] = jnp.broadcast_to(skip_ref[:, lane], (SUB, LANES))

    loads[0].wait()
    loads[1].wait()
    for t in range(TILES):
        lane = pl.ds(t * LANES, LANES)
        for n in range(SUB):
            rows = pl.ds(n * BLOCK, BLOCK)
            mix[t, pl.ds(n, BLOCK, stride=SUB), :] = (
                stage[0, rows, lane].astype(F32) * stage[1, rows, lane].astype(F32)
            )

    def states(ref, t):
        return [ref[t, m * SUB:(m + 1) * SUB, :] for m in range(MODES)]

    def scan_tile(t, carry):
        a = states(decay, t)

        def step(i, h):
            h = list(h)
            for u in range(4):
                x = mix[t, pl.ds(pl.multiple_of((i * 4 + u) * SUB, SUB), SUB), :]
                h = [a[m] * h[m] + x for m in range(MODES)]
            return tuple(h)

        zero = tuple(jnp.zeros((SUB, LANES), F32) for _ in range(MODES))
        h = lax.fori_loop(0, BLOCK // 4, step, zero)
        for m in range(MODES):
            local[t, m * SUB:(m + 1) * SUB, :] = h[m]
        return carry

    lax.fori_loop(0, TILES, scan_tile, 0)

    for t in range(TILES):
        lane = slice(t * LANES, (t + 1) * LANES)
        state = jnp.zeros((MODES, LANES), F32)
        for n in range(SUB):
            begin[t, pl.ds(n, MODES, stride=SUB), :] = state
            state = block_decay[:, lane] * state + local[t, pl.ds(n, MODES, stride=SUB), :]
        ends[0, :, lane] = state

    def state_copy(k):
        return remote(ends.at[0], ends.at[k], st_s.at[k], st_r.at[k], later(k))

    for k in range(1, 8):
        state_copy(k).start()
    for d, c in ((1, 0), (1, 1), (3, 0), (3, 1), (0, 1)):
        w_x(d, c).start()

    loads[2].wait()
    for t in range(TILES):
        lane = pl.ds(t * LANES, LANES)
        for n in range(SUB):
            gate[t, pl.ds(n, BLOCK, stride=SUB), :] = (
                stage[2, pl.ds(n * BLOCK, BLOCK), lane].astype(F32)
            )

    def pass_on(d):
        for c in (0, 1):
            w_x(d, c).wait_recv()
            w_y(d, c).start()

    for k in range(1, 8):
        state_copy(k).wait_recv()
    pass_on(2)
    incoming = jnp.zeros((MODES, WIDTH), F32)
    for k in range(7, 0, -1):
        incoming = jnp.where(k <= seq, device_decay * incoming + ends[k], incoming)
    for n in range(SUB):
        carried = jnp.exp(-rate * (BLOCK * n)) * incoming
        for t in range(TILES):
            rows = pl.ds(n, MODES, stride=SUB)
            begin[t, rows, :] = begin[t, rows, :] + carried[:, t * LANES:(t + 1) * LANES]

    def chunk_rows(r):
        return pl.ds(pl.multiple_of(r * CHUNK, CHUNK), CHUNK)

    def slot(s):
        return pl.ds(s * WIDTH, WIDTH)

    def g_mate(r):
        return remote(
            gat.at[chunk_rows(r), slot(0)], gat.at[chunk_rows(r), slot(1)],
            gc_s.at[r], gc_r.at[r], mate,
        )

    def g_x(r):
        return remote(
            gat.at[chunk_rows(r), slot(0)], gat.at[chunk_rows(r), slot(2)],
            gx_s.at[r], gx_r.at[r], x_side(0, 0),
        )

    def g_pass(r):
        return remote(
            gat.at[chunk_rows(r), slot(2)], gat.at[chunk_rows(r), slot(3)],
            gf_s.at[r], gf_r.at[r], mate,
        )

    def filter_tile(r, t):
        a = states(decay, t)
        b = states(coef, t)
        direct = skips[t, :, :]

        def step(i, h):
            h = list(h)
            parts = []
            base = r * CHUNK + i * (2 * SUB)
            for u in range(2):
                rows = pl.ds(pl.multiple_of(base + u * SUB, SUB), SUB)
                x = mix[t, rows, :]
                h = [a[m] * h[m] + x for m in range(MODES)]
                terms = [b[m] * h[m] for m in range(MODES)]
                while len(terms) > 1:
                    terms = [terms[j] + terms[j + 1] for j in range(0, len(terms), 2)]
                parts.append(gate[t, rows, :] * (terms[0] + direct * x))
            gat[
                pl.ds(pl.multiple_of(base, 2 * SUB), 2 * SUB),
                pl.ds(pl.multiple_of(t * LANES, LANES), LANES),
            ] = jnp.concatenate(parts, axis=0).astype(BF16)
            return tuple(h)

        h = lax.fori_loop(0, CHUNK // (2 * SUB), step, tuple(states(begin, t)))
        for m in range(MODES):
            begin[t, m * SUB:(m + 1) * SUB, :] = h[m]

    def filter_chunk(r, carry):
        def tile(t, carry):
            filter_tile(r, t)
            return carry

        lax.fori_loop(0, TILES, tile, 0)
        g_x(r).start()
        g_mate(r).start()
        return carry

    lax.fori_loop(0, CHUNKS, filter_chunk, 0)
    w_x(0, 0).start()
    pass_on(1)

    def w_ready(d):
        for c in (0, 1):
            w_y(d, c).wait_recv()
        w_mate(d).wait_recv()
        w_own(d).wait()

    def product(r, d):
        return jnp.dot(gat[chunk_rows(r), :], wn[d], preferred_element_type=F32)

    def first_copy(r, side):
        part = pl.ds(side * half, half)
        return remote(
            first_out.at[chunk_rows(r), part], first_in.at[chunk_rows(r), part],
            f_s.at[side, r], f_r.at[side, r], z_down if side else z_up,
        )

    def second_copy(r, side):
        return remote(
            second_out.at[side, chunk_rows(r)], second_in.at[side, chunk_rows(r)],
            s_s.at[side, r], s_r.at[side, r], z_down if side else z_up,
        )

    def first_sum(r):
        g_x(r).wait_recv()
        g_pass(r).start()
        g_mate(r).wait_recv()
        g_pass(r).wait_recv()
        first_out[chunk_rows(r), :] = product(r, 2).astype(BF16)
        for side in (0, 1):
            first_copy(r, side).start()

    def second_sum(r, side):
        part = pl.ds(side * half, half)
        rest = pl.ds((1 - side) * half, half)
        partial = product(r, 3 if side else 1)
        first_copy(r, side).wait_recv()
        summed = partial[:, side * half:(side + 1) * half] + first_in[chunk_rows(r), part].astype(F32)
        second_out[side, chunk_rows(r), part] = summed.astype(BF16)
        second_out[side, chunk_rows(r), rest] = partial[:, (1 - side) * half:(2 - side) * half].astype(BF16)
        second_copy(r, side).start()

    def last_sum(r):
        own = product(r, 0)
        for side in (0, 1):
            second_copy(r, side).wait_recv()
        own = own + second_in[0, chunk_rows(r), :].astype(F32) + second_in[1, chunk_rows(r), :].astype(F32)
        for t in range(TILES):
            total[t, :, :] = own[:, t * LANES:(t + 1) * LANES]
        piece = CHUNK // SUB
        for n in range(SUB):
            rows = pl.ds(pl.multiple_of(n * BLOCK + r * piece, piece), piece)
            for t in range(TILES):
                out_ref[rows, t * LANES:(t + 1) * LANES] = (
                    total[t, pl.ds(n, piece, stride=SUB), :].astype(BF16)
                )

    def turn(i, carry):
        @pl.when(i == 0)
        def _():
            w_ready(2)

        @pl.when(i < CHUNKS)
        def _():
            first_sum(i)

        @pl.when(i == LAG_UP)
        def _():
            w_ready(1)

        @pl.when((i >= LAG_UP) & (i < CHUNKS + LAG_UP))
        def _():
            second_sum(i - LAG_UP, 0)

        @pl.when(i == LAG_DOWN - 2)
        def _():
            pass_on(3)

        @pl.when(i == LAG_DOWN)
        def _():
            w_ready(3)

        @pl.when((i >= LAG_DOWN) & (i < CHUNKS + LAG_DOWN))
        def _():
            second_sum(i - LAG_DOWN, 1)

        @pl.when(i == LAG_LAST - 1)
        def _():
            pass_on(0)

        @pl.when(i == LAG_LAST)
        def _():
            w_ready(0)

        @pl.when(i >= LAG_LAST)
        def _():
            last_sum(i - LAG_LAST)

        return carry

    lax.fori_loop(0, CHUNKS + LAG_LAST, turn, 0)

    for d in ORDER:
        for c in (0, 1):
            w_x(d, c).wait_send()
            w_y(d, c).wait_send()
        w_mate(d).wait_send()
    for k in range(1, 8):
        state_copy(k).wait_send()

    def finish(r, carry):
        g_x(r).wait_send()
        g_mate(r).wait_send()
        g_pass(r).wait_send()
        for side in (0, 1):
            first_copy(r, side).wait_send()
            second_copy(r, side).wait_send()
        return carry

    lax.fori_loop(0, CHUNKS, finish, 0)


def local(query_rows, key_rows, value_rows, horizon, residue, skip, w_out):
    dma = pltpu.SemaphoreType.DMA
    hbm = pl.BlockSpec(memory_space=pltpu.HBM)
    vmem = pl.BlockSpec(memory_space=pltpu.VMEM)
    return pl.pallas_call(
        kernel,
        out_shape=jax.ShapeDtypeStruct((ROWS, WIDTH), BF16),
        in_specs=[hbm] * 7,
        out_specs=vmem,
        scratch_shapes=[
            pltpu.VMEM((3, ROWS, WIDTH), BF16),
            pltpu.VMEM((MODES, WIDTH), F32),
            pltpu.VMEM((MODES, WIDTH), F32),
            pltpu.VMEM((1, WIDTH), F32),
            pltpu.VMEM((TILES, ROWS, LANES), F32),
            pltpu.VMEM((TILES, ROWS, LANES), F32),
            pltpu.VMEM((TILES, MODES * SUB, LANES), F32),
            pltpu.VMEM((TILES, MODES * SUB, LANES), F32),
            pltpu.VMEM((TILES, SUB, LANES), F32),
            pltpu.VMEM((TILES, MODES * SUB, LANES), F32),
            pltpu.VMEM((TILES, MODES * SUB, LANES), F32),
            pltpu.VMEM((8, MODES, WIDTH), F32),
            pltpu.VMEM((ROWS, 4 * WIDTH), BF16),
            pltpu.VMEM((4, 4 * WIDTH, WIDTH), BF16),
            pltpu.VMEM((ROWS, WIDTH), BF16),
            pltpu.VMEM((ROWS, WIDTH), BF16),
            pltpu.VMEM((2, ROWS, WIDTH), BF16),
            pltpu.VMEM((2, ROWS, WIDTH), BF16),
            pltpu.VMEM((TILES, CHUNK, LANES), F32),
            dma((3,)), dma((3,)), dma((4,)), dma((4,)), dma((4,)),
            dma((4, 2)), dma((4, 2)), dma((4, 2)), dma((4, 2)),
            dma((8,)), dma((8,)),
            dma((CHUNKS,)), dma((CHUNKS,)), dma((CHUNKS,)), dma((CHUNKS,)),
            dma((CHUNKS,)), dma((CHUNKS,)),
            dma((2, CHUNKS)), dma((2, CHUNKS)), dma((2, CHUNKS)), dma((2, CHUNKS)),
        ],
        compiler_params=pltpu.CompilerParams(
            collective_id=0, has_side_effects=True, vmem_limit_bytes=48 << 20
        ),
        cost_estimate=pl.CostEstimate(
            flops=2 * ROWS * 16 * WIDTH * WIDTH, bytes_accessed=13 << 20, transcendentals=0
        ),
        name="layer",
    )(query_rows, key_rows, value_rows, horizon, residue, skip.reshape(1, WIDTH), w_out)


def solution(mesh):
    in_specs = (
        P("seq", "chan"),
        P("seq", "chan"),
        P("seq", "chan"),
        P(None, "chan"),
        P(None, "chan"),
        P("chan"),
        P("chan", None),
    )
    out_specs = P("seq", "chan")
    return jax.shard_map(local, mesh=mesh, in_specs=in_specs, out_specs=out_specs, check_vma=False)
```

```python
import functools

import jax
import jax.numpy as jnp
from jax import lax
from jax.experimental import pallas as pl
from jax.experimental.pallas import tpu as pltpu
from jax.sharding import PartitionSpec as P

MESH = pl.DeviceIdType.MESH
F32 = jnp.float32
BF16 = jnp.bfloat16

ROWS = 1024
WIDTH = 512
MODES = 16
SUB = 8
BLOCK = ROWS // SUB
LANES = 128
TILES = WIDTH // LANES
CHUNKS = 8
CHUNK = ROWS // CHUNKS
EARLY = 6
UP = 2
DOWN = 6
VIA = {2: (0, 1), 1: (0, 1), 3: (1, 1), 0: (1, 1)}
ORDER = (2, 1, 3, 0)


def place(y, xh, xl, z, core):
    return {"seq": y * 2 + xh, "chan": xl * 8 + z * 2 + core}


def kernel(
    q_hbm, k_hbm, v_hbm, horizon_hbm, residue_hbm, skip_hbm, w_hbm, out_ref,
    stage, horizon_ref, residue_ref, skip_ref, mix, gate, decay, coef, skips, local, begin, ends, gat, wn,
    first_out, first_in, second_out, second_in, total,
    stage_sem, small_sem, wl, wc_s, wc_r, wx_s, wx_r, wy_s, wy_r, st_s, st_r,
    gc_s, gc_r, gx_s, gx_r, gf_s, gf_r, f_s, f_r, s_s, s_r,
):
    seq = lax.axis_index("seq")
    chan = lax.axis_index("chan")
    y, xh = seq // 2, lax.rem(seq, 2)
    xl, z, core = chan // 8, lax.rem(chan // 2, 4), lax.rem(chan, 2)
    parity = lax.rem(y, 2)

    def later(k):
        return {"seq": lax.rem(seq + k, 8), "chan": chan}

    def x_side(hi, c):
        other = lax.rem(core + c, 2)
        return place(y, (1 - xh) if hi else xh, 1 - xl, z, other)

    mate = place(y, xh, xl, z, 1 - core)
    z_up = place(y, xh, xl, lax.rem(z + 1, 4), core)
    z_down = place(y, xh, xl, lax.rem(z + 3, 4), core)
    y_up = place(lax.rem(y + 1, 4), xh, xl, z, core)
    y_down = place(lax.rem(y + 3, 4), xh, xl, z, core)

    barrier = pltpu.get_barrier_semaphore()
    peers = [later(k) for k in range(1, 8)]
    peers += [mate, z_up, z_down]
    peers += [x_side(hi, c) for hi in (0, 1) for c in (0, 1)]
    for peer in peers:
        pl.semaphore_signal(barrier, inc=1, device_id=peer, device_id_type=MESH)

    loads = [
        pltpu.make_async_copy(src, stage.at[i], stage_sem.at[i])
        for i, src in enumerate((k_hbm, v_hbm, q_hbm))
    ]
    small = [
        pltpu.make_async_copy(src, dst, small_sem.at[i])
        for i, (src, dst) in enumerate(
            ((horizon_hbm, horizon_ref), (residue_hbm, residue_ref), (skip_hbm, skip_ref))
        )
    ]
    for load in small + loads:
        load.start()

    def remote(src, dst, send, recv, device):
        return pltpu.make_async_remote_copy(
            src_ref=src, dst_ref=dst, send_sem=send, recv_sem=recv,
            device_id=device, device_id_type=MESH,
        )

    def columns(a, d, b):
        block = a * 8 + lax.rem(z + d, 4) * 2 + b
        return pl.ds(pl.multiple_of(block * WIDTH, WIDTH), WIDTH)

    half = WIDTH // 2

    def half_rows(c, p):
        return pl.ds(pl.multiple_of((2 + c) * WIDTH + p * half, half), half)

    def w_x(d, c):
        return remote(
            w_hbm.at[pl.ds(pl.multiple_of(parity * half, half), half),
                     columns(1 - xl, d, lax.rem(core + c, 2))],
            wn.at[d, half_rows(c, parity)],
            wx_s.at[d, c], wx_r.at[d, c], x_side(VIA[d][c], c),
        )

    def w_y(d, c):
        piece = wn.at[d, half_rows(c, parity)]
        return remote(piece, piece, wy_s.at[d, c], wy_r.at[d, c], y_up if c else y_down)

    def w_mate(d):
        return remote(
            w_hbm.at[:, columns(xl, d, 1 - core)],
            wn.at[d, pl.ds(WIDTH, WIDTH)],
            wc_s.at[d], wc_r.at[d], mate,
        )

    def w_own(d):
        return pltpu.make_async_copy(
            w_hbm.at[:, columns(xl, d, core)], wn.at[d, pl.ds(0, WIDTH)], wl.at[d]
        )

    pl.semaphore_wait(barrier, len(peers))
    for c in (0, 1):
        w_x(2, c).start()
    for d in ORDER:
        w_mate(d).start()
    for d in ORDER:
        w_own(d).start()

    for load in small:
        load.wait()
    rate = 1.0 / horizon_ref[...]
    twice = 2.0 * rate
    series = jnp.ones_like(twice)
    for n in range(13, 1, -1):
        series = 1.0 - (twice * (1.0 / n)) * series
    power = jnp.where(twice < 0.5, twice * series, 1.0 - jnp.exp(-twice))
    scaled = residue_ref[...] * jnp.sqrt(power)
    step_decay = jnp.exp(-rate)
    block_decay = jnp.exp(-rate * BLOCK)
    device_decay = jnp.exp(-rate * ROWS)
    for t in range(TILES):
        lane = slice(t * LANES, (t + 1) * LANES)
        for m in range(MODES):
            rows = slice(m * SUB, (m + 1) * SUB)
            decay[t, rows, :] = jnp.broadcast_to(step_decay[m:m + 1, lane], (SUB, LANES))
            coef[t, rows, :] = jnp.broadcast_to(scaled[m:m + 1, lane], (SUB, LANES))
        skips[t, :, :] = jnp.broadcast_to(skip_ref[:, lane], (SUB, LANES))

    loads[0].wait()
    loads[1].wait()
    for t in range(TILES):
        lane = pl.ds(t * LANES, LANES)
        for n in range(SUB):
            rows = pl.ds(n * BLOCK, BLOCK)
            mix[t, pl.ds(n, BLOCK, stride=SUB), :] = (
                stage[0, rows, lane].astype(F32) * stage[1, rows, lane].astype(F32)
            )

    def states(ref, t):
        return [ref[t, m * SUB:(m + 1) * SUB, :] for m in range(MODES)]

    def scan_tile(t, carry):
        a = states(decay, t)

        def step(i, h):
            h = list(h)
            for u in range(4):
                x = mix[t, pl.ds(pl.multiple_of((i * 4 + u) * SUB, SUB), SUB), :]
                h = [a[m] * h[m] + x for m in range(MODES)]
            return tuple(h)

        zero = tuple(jnp.zeros((SUB, LANES), F32) for _ in range(MODES))
        h = lax.fori_loop(0, BLOCK // 4, step, zero)
        for m in range(MODES):
            local[t, m * SUB:(m + 1) * SUB, :] = h[m]
        return carry

    lax.fori_loop(0, TILES, scan_tile, 0)

    for t in range(TILES):
        lane = slice(t * LANES, (t + 1) * LANES)
        state = jnp.zeros((MODES, LANES), F32)
        for n in range(SUB):
            begin[t, pl.ds(n, MODES, stride=SUB), :] = state
            state = block_decay[:, lane] * state + local[t, pl.ds(n, MODES, stride=SUB), :]
        ends[0, :, lane] = state

    def state_copy(k):
        return remote(ends.at[0], ends.at[k], st_s.at[k], st_r.at[k], later(k))

    for k in range(1, 8):
        state_copy(k).start()
    for d, c in ((1, 0), (1, 1), (3, 0), (3, 1), (0, 0), (0, 1)):
        w_x(d, c).start()

    loads[2].wait()
    for t in range(TILES):
        lane = pl.ds(t * LANES, LANES)
        for n in range(SUB):
            gate[t, pl.ds(n, BLOCK, stride=SUB), :] = (
                stage[2, pl.ds(n * BLOCK, BLOCK), lane].astype(F32)
            )

    def pass_on(d, c):
        w_x(d, c).wait_recv()
        w_y(d, c).start()

    for k in range(1, 8):
        state_copy(k).wait_recv()
    pass_on(2, 0)
    pass_on(2, 1)
    incoming = jnp.zeros((MODES, WIDTH), F32)
    for k in range(7, 0, -1):
        incoming = jnp.where(k <= seq, device_decay * incoming + ends[k], incoming)
    for n in range(SUB):
        carried = jnp.exp(-rate * (BLOCK * n)) * incoming
        for t in range(TILES):
            rows = pl.ds(n, MODES, stride=SUB)
            begin[t, rows, :] = begin[t, rows, :] + carried[:, t * LANES:(t + 1) * LANES]

    def chunk_rows(r):
        return pl.ds(pl.multiple_of(r * CHUNK, CHUNK), CHUNK)

    def slot(s):
        return pl.ds(s * WIDTH, WIDTH)

    def g_mate(r):
        return remote(
            gat.at[chunk_rows(r), slot(0)], gat.at[chunk_rows(r), slot(1)],
            gc_s.at[r], gc_r.at[r], mate,
        )

    def g_x(r):
        return remote(
            gat.at[chunk_rows(r), slot(0)], gat.at[chunk_rows(r), slot(2)],
            gx_s.at[r], gx_r.at[r], x_side(0, 0),
        )

    def g_pass(r):
        return remote(
            gat.at[chunk_rows(r), slot(2)], gat.at[chunk_rows(r), slot(3)],
            gf_s.at[r], gf_r.at[r], mate,
        )

    def filter_tile(r, t):
        a = states(decay, t)
        b = states(coef, t)
        direct = skips[t, :, :]

        def step(i, h):
            h = list(h)
            parts = []
            base = r * CHUNK + i * (2 * SUB)
            for u in range(2):
                rows = pl.ds(pl.multiple_of(base + u * SUB, SUB), SUB)
                x = mix[t, rows, :]
                h = [a[m] * h[m] + x for m in range(MODES)]
                terms = [b[m] * h[m] for m in range(MODES)]
                while len(terms) > 1:
                    terms = [terms[j] + terms[j + 1] for j in range(0, len(terms), 2)]
                parts.append(gate[t, rows, :] * (terms[0] + direct * x))
            gat[
                pl.ds(pl.multiple_of(base, 2 * SUB), 2 * SUB),
                pl.ds(pl.multiple_of(t * LANES, LANES), LANES),
            ] = jnp.concatenate(parts, axis=0).astype(BF16)
            return tuple(h)

        h = lax.fori_loop(0, CHUNK // (2 * SUB), step, tuple(states(begin, t)))
        for m in range(MODES):
            begin[t, m * SUB:(m + 1) * SUB, :] = h[m]

    def filter_chunk(r, carry):
        def tile(t, carry):
            filter_tile(r, t)
            return carry

        lax.fori_loop(0, TILES, tile, 0)
        g_x(r).start()
        g_mate(r).start()
        return carry

    lax.fori_loop(0, CHUNKS, filter_chunk, 0)
    pass_on(1, 0)
    pass_on(1, 1)

    def w_ready(d):
        for c in (0, 1):
            w_y(d, c).wait_recv()
        w_mate(d).wait_recv()
        w_own(d).wait()

    def product(r, d):
        return jnp.dot(gat[chunk_rows(r), :], wn[d], preferred_element_type=F32)

    def first_copy(r, device):
        return remote(
            first_out.at[chunk_rows(r)], first_in.at[chunk_rows(r)], f_s.at[r], f_r.at[r], device
        )

    def second_copy(r, side):
        return remote(
            second_out.at[side, chunk_rows(r)], second_in.at[side, chunk_rows(r)],
            s_s.at[side, r], s_r.at[side, r], z_down if side else z_up,
        )

    def first_sum(r):
        g_x(r).wait_recv()
        g_pass(r).start()
        g_mate(r).wait_recv()
        g_pass(r).wait_recv()
        first_out[chunk_rows(r), :] = product(r, 2).astype(BF16)

        @pl.when(r < EARLY)
        def _():
            first_copy(r, z_down).start()

        @pl.when(r >= EARLY)
        def _():
            first_copy(r, z_up).start()

    def second_sum(r, side):
        partial = product(r, 3 if side else 1)
        passes = r < EARLY if side else r >= EARLY

        @pl.when(passes)
        def _():
            first_copy(r, z_up).wait_recv()
            second_out[side, chunk_rows(r), :] = (
                partial + first_in[chunk_rows(r), :].astype(F32)
            ).astype(BF16)

        @pl.when(jnp.logical_not(passes))
        def _():
            second_out[side, chunk_rows(r), :] = partial.astype(BF16)

        second_copy(r, side).start()

    def last_sum(r):
        own = product(r, 0)
        for side in (0, 1):
            second_copy(r, side).wait_recv()
        own = own + second_in[0, chunk_rows(r), :].astype(F32) + second_in[1, chunk_rows(r), :].astype(F32)
        for t in range(TILES):
            total[t, :, :] = own[:, t * LANES:(t + 1) * LANES]
        piece = CHUNK // SUB
        for n in range(SUB):
            rows = pl.ds(pl.multiple_of(n * BLOCK + r * piece, piece), piece)
            for t in range(TILES):
                out_ref[rows, t * LANES:(t + 1) * LANES] = (
                    total[t, pl.ds(n, piece, stride=SUB), :].astype(BF16)
                )

    def between(first, last, body):
        def step(r, carry):
            body(r)
            return carry

        lax.fori_loop(first, last, step, 0)

    def turn(i, carry):
        for at, d, c in ((2, 3, 0), (4, 3, 1), (6, 0, 0)):
            @pl.when(i == at)
            def _(d=d, c=c):
                pass_on(d, c)

        @pl.when(i == 0)
        def _():
            w_ready(2)

        first_sum(i)

        for at, d in ((UP, 1), (DOWN, 3)):
            @pl.when(i == at)
            def _(d=d):
                w_ready(d)

        upward = (i >= UP) & (i < EARLY)
        between(jnp.where(i == UP, 0, i), jnp.where(upward, i + 1, 0), lambda r: second_sum(r, 0))
        downward = 2 * jnp.maximum(i - DOWN, 0)
        between(downward, jnp.where(i < DOWN, 0, downward + 2), lambda r: second_sum(r, 1))
        return carry

    lax.fori_loop(0, CHUNKS, turn, 0)
    pass_on(0, 1)
    between(2 * (CHUNKS - DOWN), CHUNKS, lambda r: second_sum(r, 1))
    between(EARLY, CHUNKS, lambda r: second_sum(r, 0))
    w_ready(0)
    between(0, CHUNKS, last_sum)

    for d in ORDER:
        for c in (0, 1):
            w_x(d, c).wait_send()
            w_y(d, c).wait_send()
        w_mate(d).wait_send()
    for k in range(1, 8):
        state_copy(k).wait_send()

    def finish(r, carry):
        g_x(r).wait_send()
        g_mate(r).wait_send()
        g_pass(r).wait_send()
        first_copy(r, z_up).wait_send()
        for side in (0, 1):
            second_copy(r, side).wait_send()
        return carry

    lax.fori_loop(0, CHUNKS, finish, 0)


def local(query_rows, key_rows, value_rows, horizon, residue, skip, w_out):
    dma = pltpu.SemaphoreType.DMA
    hbm = pl.BlockSpec(memory_space=pltpu.HBM)
    vmem = pl.BlockSpec(memory_space=pltpu.VMEM)
    return pl.pallas_call(
        kernel,
        out_shape=jax.ShapeDtypeStruct((ROWS, WIDTH), BF16),
        in_specs=[hbm] * 7,
        out_specs=vmem,
        scratch_shapes=[
            pltpu.VMEM((3, ROWS, WIDTH), BF16),
            pltpu.VMEM((MODES, WIDTH), F32),
            pltpu.VMEM((MODES, WIDTH), F32),
            pltpu.VMEM((1, WIDTH), F32),
            pltpu.VMEM((TILES, ROWS, LANES), F32),
            pltpu.VMEM((TILES, ROWS, LANES), F32),
            pltpu.VMEM((TILES, MODES * SUB, LANES), F32),
            pltpu.VMEM((TILES, MODES * SUB, LANES), F32),
            pltpu.VMEM((TILES, SUB, LANES), F32),
            pltpu.VMEM((TILES, MODES * SUB, LANES), F32),
            pltpu.VMEM((TILES, MODES * SUB, LANES), F32),
            pltpu.VMEM((8, MODES, WIDTH), F32),
            pltpu.VMEM((ROWS, 4 * WIDTH), BF16),
            pltpu.VMEM((4, 4 * WIDTH, WIDTH), BF16),
            pltpu.VMEM((ROWS, WIDTH), BF16),
            pltpu.VMEM((ROWS, WIDTH), BF16),
            pltpu.VMEM((2, ROWS, WIDTH), BF16),
            pltpu.VMEM((2, ROWS, WIDTH), BF16),
            pltpu.VMEM((TILES, CHUNK, LANES), F32),
            dma((3,)), dma((3,)), dma((4,)), dma((4,)), dma((4,)),
            dma((4, 2)), dma((4, 2)), dma((4, 2)), dma((4, 2)),
            dma((8,)), dma((8,)),
            dma((CHUNKS,)), dma((CHUNKS,)), dma((CHUNKS,)), dma((CHUNKS,)),
            dma((CHUNKS,)), dma((CHUNKS,)),
            dma((CHUNKS,)), dma((CHUNKS,)), dma((2, CHUNKS)), dma((2, CHUNKS)),
        ],
        compiler_params=pltpu.CompilerParams(
            collective_id=0, has_side_effects=True, vmem_limit_bytes=60 << 20
        ),
        cost_estimate=pl.CostEstimate(
            flops=2 * ROWS * 16 * WIDTH * WIDTH, bytes_accessed=13 << 20, transcendentals=0
        ),
        name="layer",
    )(query_rows, key_rows, value_rows, horizon, residue, skip.reshape(1, WIDTH), w_out)


def solution(mesh):
    in_specs = (
        P("seq", "chan"),
        P("seq", "chan"),
        P("seq", "chan"),
        P(None, "chan"),
        P(None, "chan"),
        P("chan"),
        P("chan", None),
    )
    out_specs = P("seq", "chan")
    return jax.shard_map(local, mesh=mesh, in_specs=in_specs, out_specs=out_specs, check_vma=False)
```

```python
import functools

import jax
import jax.numpy as jnp
from jax import lax
from jax.experimental import pallas as pl
from jax.experimental.pallas import tpu as pltpu
from jax.sharding import PartitionSpec as P

MESH = pl.DeviceIdType.MESH
F32 = jnp.float32
BF16 = jnp.bfloat16

ROWS = 1024
WIDTH = 512
MODES = 16
SUB = 8
BLOCK = ROWS // SUB
LANES = 128
TILES = WIDTH // LANES
CHUNKS = 8
CHUNK = ROWS // CHUNKS
EARLY = 5
UP = 2
DOWN = 6
VIA = {2: (0, 1), 1: (0, 1), 3: (1, 1), 0: (1, 1)}
ORDER = (2, 1, 3, 0)


def place(y, xh, xl, z, core):
    return {"seq": y * 2 + xh, "chan": xl * 8 + z * 2 + core}


def kernel(
    q_hbm, k_hbm, v_hbm, horizon_hbm, residue_hbm, skip_hbm, w_hbm, out_ref,
    stage, horizon_ref, residue_ref, skip_ref, mix, gate, decay, coef, skips, local, begin, ends, gat, wn,
    first_out, first_in, second_out, second_in, near, total,
    stage_sem, small_sem, wl, wc_s, wc_r, wx_s, wx_r, wy_s, wy_r, st_s, st_r,
    gc_s, gc_r, gx_s, gx_r, gf_s, gf_r, f_s, f_r, s_s, s_r,
):
    seq = lax.axis_index("seq")
    chan = lax.axis_index("chan")
    y, xh = seq // 2, lax.rem(seq, 2)
    xl, z, core = chan // 8, lax.rem(chan // 2, 4), lax.rem(chan, 2)
    parity = lax.rem(y, 2)

    def later(k):
        return {"seq": lax.rem(seq + k, 8), "chan": chan}

    def x_side(hi, c):
        other = lax.rem(core + c, 2)
        return place(y, (1 - xh) if hi else xh, 1 - xl, z, other)

    mate = place(y, xh, xl, z, 1 - core)
    z_up = place(y, xh, xl, lax.rem(z + 1, 4), core)
    z_down = place(y, xh, xl, lax.rem(z + 3, 4), core)
    y_up = place(lax.rem(y + 1, 4), xh, xl, z, core)
    y_down = place(lax.rem(y + 3, 4), xh, xl, z, core)

    barrier = pltpu.get_barrier_semaphore()
    peers = [later(k) for k in range(1, 8)]
    peers += [mate, z_up, z_down]
    peers += [x_side(hi, c) for hi in (0, 1) for c in (0, 1)]
    for peer in peers:
        pl.semaphore_signal(barrier, inc=1, device_id=peer, device_id_type=MESH)

    loads = [
        pltpu.make_async_copy(src, stage.at[i], stage_sem.at[i])
        for i, src in enumerate((k_hbm, v_hbm, q_hbm))
    ]
    small = [
        pltpu.make_async_copy(src, dst, small_sem.at[i])
        for i, (src, dst) in enumerate(
            ((horizon_hbm, horizon_ref), (residue_hbm, residue_ref), (skip_hbm, skip_ref))
        )
    ]
    for load in small + loads:
        load.start()

    def remote(src, dst, send, recv, device):
        return pltpu.make_async_remote_copy(
            src_ref=src, dst_ref=dst, send_sem=send, recv_sem=recv,
            device_id=device, device_id_type=MESH,
        )

    def columns(a, d, b):
        block = a * 8 + lax.rem(z + d, 4) * 2 + b
        return pl.ds(pl.multiple_of(block * WIDTH, WIDTH), WIDTH)

    half = WIDTH // 2
    part = half // 2

    def part_rows(first, h):
        return pl.ds(pl.multiple_of(first + parity * half + h * part, part), part)

    def w_x(d, c, h):
        return remote(
            w_hbm.at[part_rows(0, h), columns(1 - xl, d, lax.rem(core + c, 2))],
            wn.at[d, part_rows((2 + c) * WIDTH, h)],
            wx_s.at[d, c, h], wx_r.at[d, c, h], x_side(VIA[d][c], c),
        )

    def w_y(d, c, h):
        piece = wn.at[d, part_rows((2 + c) * WIDTH, h)]
        return remote(piece, piece, wy_s.at[d, c, h], wy_r.at[d, c, h], y_up if c else y_down)

    def w_mate(d):
        return remote(
            w_hbm.at[:, columns(xl, d, 1 - core)],
            wn.at[d, pl.ds(WIDTH, WIDTH)],
            wc_s.at[d], wc_r.at[d], mate,
        )

    def w_own(d):
        return pltpu.make_async_copy(
            w_hbm.at[:, columns(xl, d, core)], wn.at[d, pl.ds(0, WIDTH)], wl.at[d]
        )

    pl.semaphore_wait(barrier, len(peers))
    for c in (0, 1):
        for h in (0, 1):
            w_x(2, c, h).start()
    for d in ORDER:
        w_mate(d).start()
    for d in ORDER:
        w_own(d).start()

    for load in small:
        load.wait()
    rate = 1.0 / horizon_ref[...]
    twice = 2.0 * rate
    series = jnp.ones_like(twice)
    for n in range(13, 1, -1):
        series = 1.0 - (twice * (1.0 / n)) * series
    power = jnp.where(twice < 0.5, twice * series, 1.0 - jnp.exp(-twice))
    scaled = residue_ref[...] * jnp.sqrt(power)
    step_decay = jnp.exp(-rate)
    block_decay = jnp.exp(-rate * BLOCK)
    device_decay = jnp.exp(-rate * ROWS)
    for t in range(TILES):
        lane = slice(t * LANES, (t + 1) * LANES)
        for m in range(MODES):
            rows = slice(m * SUB, (m + 1) * SUB)
            decay[t, rows, :] = jnp.broadcast_to(step_decay[m:m + 1, lane], (SUB, LANES))
            coef[t, rows, :] = jnp.broadcast_to(scaled[m:m + 1, lane], (SUB, LANES))
        skips[t, :, :] = jnp.broadcast_to(skip_ref[:, lane], (SUB, LANES))

    loads[0].wait()
    loads[1].wait()
    for t in range(TILES):
        lane = pl.ds(t * LANES, LANES)
        for n in range(SUB):
            rows = pl.ds(n * BLOCK, BLOCK)
            mix[t, pl.ds(n, BLOCK, stride=SUB), :] = (
                stage[0, rows, lane].astype(F32) * stage[1, rows, lane].astype(F32)
            )

    def states(ref, t):
        return [ref[t, m * SUB:(m + 1) * SUB, :] for m in range(MODES)]

    def scan_tile(t, carry):
        a = states(decay, t)

        def step(i, h):
            h = list(h)
            for u in range(4):
                x = mix[t, pl.ds(pl.multiple_of((i * 4 + u) * SUB, SUB), SUB), :]
                h = [a[m] * h[m] + x for m in range(MODES)]
            return tuple(h)

        zero = tuple(jnp.zeros((SUB, LANES), F32) for _ in range(MODES))
        h = lax.fori_loop(0, BLOCK // 4, step, zero)
        for m in range(MODES):
            local[t, m * SUB:(m + 1) * SUB, :] = h[m]
        return carry

    lax.fori_loop(0, TILES, scan_tile, 0)

    for t in range(TILES):
        lane = slice(t * LANES, (t + 1) * LANES)
        state = jnp.zeros((MODES, LANES), F32)
        for n in range(SUB):
            begin[t, pl.ds(n, MODES, stride=SUB), :] = state
            state = block_decay[:, lane] * state + local[t, pl.ds(n, MODES, stride=SUB), :]
        ends[0, :, lane] = state

    def state_copy(k):
        return remote(ends.at[0], ends.at[k], st_s.at[k], st_r.at[k], later(k))

    for k in range(1, 8):
        state_copy(k).start()
    for d, c in ((1, 0), (1, 1), (3, 0), (3, 1), (0, 0), (0, 1)):
        for h in (0, 1):
            w_x(d, c, h).start()

    loads[2].wait()
    for t in range(TILES):
        lane = pl.ds(t * LANES, LANES)
        for n in range(SUB):
            gate[t, pl.ds(n, BLOCK, stride=SUB), :] = (
                stage[2, pl.ds(n * BLOCK, BLOCK), lane].astype(F32)
            )

    def pass_on(d, c, parts=(0, 1)):
        for h in parts:
            w_x(d, c, h).wait_recv()
            w_y(d, c, h).start()

    for k in range(1, 8):
        state_copy(k).wait_recv()
    pass_on(2, 0)
    pass_on(2, 1)
    incoming = jnp.zeros((MODES, WIDTH), F32)
    for k in range(7, 0, -1):
        incoming = jnp.where(k <= seq, device_decay * incoming + ends[k], incoming)
    for n in range(SUB):
        carried = jnp.exp(-rate * (BLOCK * n)) * incoming
        for t in range(TILES):
            rows = pl.ds(n, MODES, stride=SUB)
            begin[t, rows, :] = begin[t, rows, :] + carried[:, t * LANES:(t + 1) * LANES]

    def chunk_rows(r):
        return pl.ds(pl.multiple_of(r * CHUNK, CHUNK), CHUNK)

    def slot(s):
        return pl.ds(s * WIDTH, WIDTH)

    def g_mate(r):
        return remote(
            gat.at[chunk_rows(r), slot(0)], gat.at[chunk_rows(r), slot(1)],
            gc_s.at[r], gc_r.at[r], mate,
        )

    def g_x(r):
        return remote(
            gat.at[chunk_rows(r), slot(0)], gat.at[chunk_rows(r), slot(2)],
            gx_s.at[r], gx_r.at[r], x_side(0, 0),
        )

    def g_pass(r):
        return remote(
            gat.at[chunk_rows(r), slot(2)], gat.at[chunk_rows(r), slot(3)],
            gf_s.at[r], gf_r.at[r], mate,
        )

    def filter_tile(r, t):
        a = states(decay, t)
        b = states(coef, t)
        direct = skips[t, :, :]

        def step(i, h):
            h = list(h)
            parts = []
            base = r * CHUNK + i * (2 * SUB)
            for u in range(2):
                rows = pl.ds(pl.multiple_of(base + u * SUB, SUB), SUB)
                x = mix[t, rows, :]
                h = [a[m] * h[m] + x for m in range(MODES)]
                terms = [b[m] * h[m] for m in range(MODES)]
                while len(terms) > 1:
                    terms = [terms[j] + terms[j + 1] for j in range(0, len(terms), 2)]
                parts.append(gate[t, rows, :] * (terms[0] + direct * x))
            gat[
                pl.ds(pl.multiple_of(base, 2 * SUB), 2 * SUB),
                pl.ds(pl.multiple_of(t * LANES, LANES), LANES),
            ] = jnp.concatenate(parts, axis=0).astype(BF16)
            return tuple(h)

        h = lax.fori_loop(0, CHUNK // (2 * SUB), step, tuple(states(begin, t)))
        for m in range(MODES):
            begin[t, m * SUB:(m + 1) * SUB, :] = h[m]

    def filter_chunk(r, carry):
        def tile(t, carry):
            filter_tile(r, t)
            return carry

        lax.fori_loop(0, TILES, tile, 0)
        g_x(r).start()
        g_mate(r).start()
        return carry

    lax.fori_loop(0, CHUNKS, filter_chunk, 0)
    pass_on(1, 0)
    pass_on(1, 1)

    def w_ready(d):
        for c in (0, 1):
            for h in (0, 1):
                w_y(d, c, h).wait_recv()

    def product(r, d):
        return jnp.dot(gat[chunk_rows(r), :], wn[d], preferred_element_type=F32)

    def near_product(b):
        rows = pl.ds(pl.multiple_of(b * 256, 256), 256)
        near[rows, :] = jnp.dot(
            gat[rows, 0:2 * WIDTH], wn[0, 0:2 * WIDTH, :], preferred_element_type=F32
        )

    def first_copy(r, device):
        return remote(
            first_out.at[chunk_rows(r)], first_in.at[chunk_rows(r)], f_s.at[r], f_r.at[r], device
        )

    def second_copy(r, side):
        return remote(
            second_out.at[side, chunk_rows(r)], second_in.at[side, chunk_rows(r)],
            s_s.at[side, r], s_r.at[side, r], z_down if side else z_up,
        )

    def first_sum(r):
        g_mate(r).wait_recv()
        g_pass(r).wait_recv()
        first_out[chunk_rows(r), :] = product(r, 2).astype(BF16)

        @pl.when(r < EARLY)
        def _():
            first_copy(r, z_down).start()

        @pl.when(r >= EARLY)
        def _():
            first_copy(r, z_up).start()

    def second_sum(r, side):
        partial = product(r, 3 if side else 1)
        passes = r < EARLY if side else r >= EARLY

        @pl.when(passes)
        def _():
            first_copy(r, z_up).wait_recv()
            second_out[side, chunk_rows(r), :] = (
                partial + first_in[chunk_rows(r), :].astype(F32)
            ).astype(BF16)

        @pl.when(jnp.logical_not(passes))
        def _():
            second_out[side, chunk_rows(r), :] = partial.astype(BF16)

        second_copy(r, side).start()

    def last_sum(r):
        own = near[chunk_rows(r), :] + jnp.dot(
            gat[chunk_rows(r), 2 * WIDTH:4 * WIDTH], wn[0, 2 * WIDTH:4 * WIDTH, :],
            preferred_element_type=F32,
        )
        for side in (0, 1):
            second_copy(r, side).wait_recv()
        own = own + second_in[0, chunk_rows(r), :].astype(F32) + second_in[1, chunk_rows(r), :].astype(F32)
        for t in range(TILES):
            total[t, :, :] = own[:, t * LANES:(t + 1) * LANES]
        piece = CHUNK // SUB
        for n in range(SUB):
            rows = pl.ds(pl.multiple_of(n * BLOCK + r * piece, piece), piece)
            for t in range(TILES):
                out_ref[rows, t * LANES:(t + 1) * LANES] = (
                    total[t, pl.ds(n, piece, stride=SUB), :].astype(BF16)
                )

    def between(first, last, body):
        def step(r, carry):
            body(r)
            return carry

        lax.fori_loop(first, last, step, 0)

    def turn(i, carry):
        for at, c, parts in ((2, 0, (0, 1)), (3, 1, (0,)), (4, 1, (1,))):
            @pl.when(i == at)
            def _(c=c, parts=parts):
                pass_on(3, c, parts)

        g_x(i).wait_recv()
        g_pass(i).start()

        for at, d in ((0, 2), (UP, 1), (DOWN, 3)):
            @pl.when(i == at)
            def _(d=d):
                w_ready(d)

        upward = (i >= UP) & (i <= EARLY)
        between(jnp.where(i == UP, 0, jnp.maximum(i - 1, 0)), jnp.where(upward, i, 0), lambda r: second_sum(r, 0))
        downward = 2 * jnp.maximum(i - DOWN, 0)
        between(downward, jnp.where(i < DOWN, 0, downward + 2), lambda r: second_sum(r, 1))
        first_sum(i)
        return carry

    for d in ORDER:
        w_mate(d).wait_recv()
        w_own(d).wait()
    lax.fori_loop(0, CHUNKS, turn, 0)
    pass_on(0, 0)
    between(2 * (CHUNKS - DOWN), CHUNKS, lambda r: second_sum(r, 1))
    pass_on(0, 1)
    between(0, ROWS // 256, near_product)
    between(EARLY, CHUNKS, lambda r: second_sum(r, 0))
    w_ready(0)
    between(0, CHUNKS, last_sum)

    for d in ORDER:
        for c in (0, 1):
            for h in (0, 1):
                w_x(d, c, h).wait_send()
                w_y(d, c, h).wait_send()
        w_mate(d).wait_send()
    for k in range(1, 8):
        state_copy(k).wait_send()

    def finish(r, carry):
        g_x(r).wait_send()
        g_mate(r).wait_send()
        g_pass(r).wait_send()
        first_copy(r, z_up).wait_send()
        for side in (0, 1):
            second_copy(r, side).wait_send()
        return carry

    lax.fori_loop(0, CHUNKS, finish, 0)


def local(query_rows, key_rows, value_rows, horizon, residue, skip, w_out):
    dma = pltpu.SemaphoreType.DMA
    hbm = pl.BlockSpec(memory_space=pltpu.HBM)
    vmem = pl.BlockSpec(memory_space=pltpu.VMEM)
    return pl.pallas_call(
        kernel,
        out_shape=pltpu.VMEM((ROWS, WIDTH), BF16),
        in_specs=[hbm] * 7,
        out_specs=vmem,
        scratch_shapes=[
            pltpu.VMEM((3, ROWS, WIDTH), BF16),
            pltpu.VMEM((MODES, WIDTH), F32),
            pltpu.VMEM((MODES, WIDTH), F32),
            pltpu.VMEM((1, WIDTH), F32),
            pltpu.VMEM((TILES, ROWS, LANES), F32),
            pltpu.VMEM((TILES, ROWS, LANES), F32),
            pltpu.VMEM((TILES, MODES * SUB, LANES), F32),
            pltpu.VMEM((TILES, MODES * SUB, LANES), F32),
            pltpu.VMEM((TILES, SUB, LANES), F32),
            pltpu.VMEM((TILES, MODES * SUB, LANES), F32),
            pltpu.VMEM((TILES, MODES * SUB, LANES), F32),
            pltpu.VMEM((8, MODES, WIDTH), F32),
            pltpu.VMEM((ROWS, 4 * WIDTH), BF16),
            pltpu.VMEM((4, 4 * WIDTH, WIDTH), BF16),
            pltpu.VMEM((ROWS, WIDTH), BF16),
            pltpu.VMEM((ROWS, WIDTH), BF16),
            pltpu.VMEM((2, ROWS, WIDTH), BF16),
            pltpu.VMEM((2, ROWS, WIDTH), BF16),
            pltpu.VMEM((ROWS, WIDTH), F32),
            pltpu.VMEM((TILES, CHUNK, LANES), F32),
            dma((3,)), dma((3,)), dma((4,)), dma((4,)), dma((4,)),
            dma((4, 2, 2)), dma((4, 2, 2)), dma((4, 2, 2)), dma((4, 2, 2)),
            dma((8,)), dma((8,)),
            dma((CHUNKS,)), dma((CHUNKS,)), dma((CHUNKS,)), dma((CHUNKS,)),
            dma((CHUNKS,)), dma((CHUNKS,)),
            dma((CHUNKS,)), dma((CHUNKS,)), dma((2, CHUNKS)), dma((2, CHUNKS)),
        ],
        compiler_params=pltpu.CompilerParams(
            collective_id=0, has_side_effects=True, vmem_limit_bytes=60 << 20
        ),
        cost_estimate=pl.CostEstimate(
            flops=2 * ROWS * 16 * WIDTH * WIDTH, bytes_accessed=13 << 20, transcendentals=0
        ),
        name="layer",
    )(query_rows, key_rows, value_rows, horizon, residue, skip.reshape(1, WIDTH), w_out)


def solution(mesh):
    in_specs = (
        P("seq", "chan"),
        P("seq", "chan"),
        P("seq", "chan"),
        P(None, "chan"),
        P(None, "chan"),
        P("chan"),
        P("chan", None),
    )
    out_specs = P("seq", "chan")
    return jax.shard_map(local, mesh=mesh, in_specs=in_specs, out_specs=out_specs, check_vma=False)
```

```python
import functools

import jax
import jax.numpy as jnp
from jax import lax
from jax.experimental import pallas as pl
from jax.experimental.pallas import tpu as pltpu
from jax.sharding import PartitionSpec as P

MESH = pl.DeviceIdType.MESH
F32 = jnp.float32
BF16 = jnp.bfloat16

ROWS = 1024
WIDTH = 512
MODES = 16
SUB = 8
BLOCK = ROWS // SUB
LANES = 128
TILES = WIDTH // LANES
CHUNKS = 8
CHUNK = ROWS // CHUNKS
EARLY = 5
UP = 2
DOWN = 6
VIA = {2: (0, 1), 1: (0, 1), 3: (1, 1), 0: (1, 1)}
ORDER = (2, 1, 3, 0)


def place(y, xh, xl, z, core):
    return {"seq": y * 2 + xh, "chan": xl * 8 + z * 2 + core}


def kernel(
    q_hbm, k_hbm, v_hbm, horizon_hbm, residue_hbm, skip_hbm, w_hbm, out_ref,
    stage, horizon_ref, residue_ref, skip_ref, mix, gate, decay, coef, skips, local, begin, ends, gat, wn,
    first_out, first_in, second_out, second_in, near, total,
    stage_sem, small_sem, wl, wc_s, wc_r, wx_s, wx_r, wy_s, wy_r, st_s, st_r,
    gc_s, gc_r, gx_s, gx_r, gf_s, gf_r, f_s, f_r, s_s, s_r,
):
    seq = lax.axis_index("seq")
    chan = lax.axis_index("chan")
    y, xh = seq // 2, lax.rem(seq, 2)
    xl, z, core = chan // 8, lax.rem(chan // 2, 4), lax.rem(chan, 2)
    parity = lax.rem(y, 2)

    def later(k):
        return {"seq": lax.rem(seq + k, 8), "chan": chan}

    def x_side(hi, c):
        other = lax.rem(core + c, 2)
        return place(y, (1 - xh) if hi else xh, 1 - xl, z, other)

    mate = place(y, xh, xl, z, 1 - core)
    z_up = place(y, xh, xl, lax.rem(z + 1, 4), core)
    z_down = place(y, xh, xl, lax.rem(z + 3, 4), core)
    y_up = place(lax.rem(y + 1, 4), xh, xl, z, core)
    y_down = place(lax.rem(y + 3, 4), xh, xl, z, core)

    barrier = pltpu.get_barrier_semaphore()
    peers = [later(k) for k in range(1, 8)]
    peers += [mate, z_up, z_down]
    peers += [x_side(hi, c) for hi in (0, 1) for c in (0, 1)]
    for peer in peers:
        pl.semaphore_signal(barrier, inc=1, device_id=peer, device_id_type=MESH)

    loads = [
        pltpu.make_async_copy(src, stage.at[i], stage_sem.at[i])
        for i, src in enumerate((k_hbm, v_hbm, q_hbm))
    ]
    small = [
        pltpu.make_async_copy(src, dst, small_sem.at[i])
        for i, (src, dst) in enumerate(
            ((horizon_hbm, horizon_ref), (residue_hbm, residue_ref), (skip_hbm, skip_ref))
        )
    ]
    for load in small + loads:
        load.start()

    def remote(src, dst, send, recv, device):
        return pltpu.make_async_remote_copy(
            src_ref=src, dst_ref=dst, send_sem=send, recv_sem=recv,
            device_id=device, device_id_type=MESH,
        )

    def columns(a, d, b):
        block = a * 8 + lax.rem(z + d, 4) * 2 + b
        return pl.ds(pl.multiple_of(block * WIDTH, WIDTH), WIDTH)

    half = WIDTH // 2
    part = half // 2

    def part_rows(first, h):
        return pl.ds(pl.multiple_of(first + parity * half + h * part, part), part)

    def w_x(d, c, h):
        return remote(
            w_hbm.at[part_rows(0, h), columns(1 - xl, d, lax.rem(core + c, 2))],
            wn.at[d, part_rows((2 + c) * WIDTH, h)],
            wx_s.at[d, c, h], wx_r.at[d, c, h], x_side(VIA[d][c], c),
        )

    def w_y(d, c, h):
        piece = wn.at[d, part_rows((2 + c) * WIDTH, h)]
        return remote(piece, piece, wy_s.at[d, c, h], wy_r.at[d, c, h], y_up if c else y_down)

    def w_mate(d):
        return remote(
            w_hbm.at[:, columns(xl, d, 1 - core)],
            wn.at[d, pl.ds(WIDTH, WIDTH)],
            wc_s.at[d], wc_r.at[d], mate,
        )

    def w_own(d):
        return pltpu.make_async_copy(
            w_hbm.at[:, columns(xl, d, core)], wn.at[d, pl.ds(0, WIDTH)], wl.at[d]
        )

    for load in small:
        load.wait()
    rate = 1.0 / horizon_ref[...]
    twice = 2.0 * rate
    series = jnp.ones_like(twice)
    for n in range(13, 1, -1):
        series = 1.0 - (twice * (1.0 / n)) * series
    power = jnp.where(twice < 0.5, twice * series, 1.0 - jnp.exp(-twice))
    scaled = residue_ref[...] * jnp.sqrt(power)
    step_decay = jnp.exp(-rate)
    block_decay = jnp.exp(-rate * BLOCK)
    device_decay = jnp.exp(-rate * ROWS)
    for t in range(TILES):
        lane = slice(t * LANES, (t + 1) * LANES)
        for m in range(MODES):
            rows = slice(m * SUB, (m + 1) * SUB)
            decay[t, rows, :] = jnp.broadcast_to(step_decay[m:m + 1, lane], (SUB, LANES))
            coef[t, rows, :] = jnp.broadcast_to(scaled[m:m + 1, lane], (SUB, LANES))
        skips[t, :, :] = jnp.broadcast_to(skip_ref[:, lane], (SUB, LANES))

    pl.semaphore_wait(barrier, len(peers))
    for c in (0, 1):
        for h in (0, 1):
            w_x(2, c, h).start()
    for d in ORDER:
        w_mate(d).start()
    for d in ORDER:
        w_own(d).start()

    loads[0].wait()
    loads[1].wait()
    for t in range(TILES):
        lane = pl.ds(t * LANES, LANES)
        for n in range(SUB):
            rows = pl.ds(n * BLOCK, BLOCK)
            mix[t, pl.ds(n, BLOCK, stride=SUB), :] = (
                stage[0, rows, lane].astype(F32) * stage[1, rows, lane].astype(F32)
            )

    def states(ref, t):
        return [ref[t, m * SUB:(m + 1) * SUB, :] for m in range(MODES)]

    def scan_tile(t, carry):
        a = states(decay, t)

        def step(i, h):
            h = list(h)
            for u in range(4):
                x = mix[t, pl.ds(pl.multiple_of((i * 4 + u) * SUB, SUB), SUB), :]
                h = [a[m] * h[m] + x for m in range(MODES)]
            return tuple(h)

        zero = tuple(jnp.zeros((SUB, LANES), F32) for _ in range(MODES))
        h = lax.fori_loop(0, BLOCK // 4, step, zero)
        for m in range(MODES):
            local[t, m * SUB:(m + 1) * SUB, :] = h[m]
        return carry

    lax.fori_loop(0, TILES, scan_tile, 0)

    for t in range(TILES):
        lane = slice(t * LANES, (t + 1) * LANES)
        state = jnp.zeros((MODES, LANES), F32)
        for n in range(SUB):
            begin[t, pl.ds(n, MODES, stride=SUB), :] = state
            state = block_decay[:, lane] * state + local[t, pl.ds(n, MODES, stride=SUB), :]
        ends[0, :, lane] = state

    def state_copy(k):
        return remote(ends.at[0], ends.at[k], st_s.at[k], st_r.at[k], later(k))

    for k in range(1, 8):
        @pl.when(seq + k < 8)
        def _(k=k):
            state_copy(k).start()

        @pl.when(k > seq)
        def _(k=k):
            ends[k, :, :] = jnp.zeros((MODES, WIDTH), F32)
    for d, c in ((1, 0), (1, 1), (3, 0), (3, 1), (0, 0), (0, 1)):
        for h in (0, 1):
            w_x(d, c, h).start()

    loads[2].wait()
    for t in range(TILES):
        lane = pl.ds(t * LANES, LANES)
        for n in range(SUB):
            gate[t, pl.ds(n, BLOCK, stride=SUB), :] = (
                stage[2, pl.ds(n * BLOCK, BLOCK), lane].astype(F32)
            )

    def pass_on(d, c, parts=(0, 1)):
        for h in parts:
            w_x(d, c, h).wait_recv()
            w_y(d, c, h).start()

    pass_on(2, 0)
    pass_on(2, 1)
    for k in range(1, 8):
        @pl.when(k <= seq)
        def _(k=k):
            state_copy(k).wait_recv()
    incoming = jnp.zeros((MODES, WIDTH), F32)
    for k in range(7, 0, -1):
        incoming = jnp.where(k <= seq, device_decay * incoming + ends[k], incoming)
    for n in range(SUB):
        carried = jnp.exp(-rate * (BLOCK * n)) * incoming
        for t in range(TILES):
            rows = pl.ds(n, MODES, stride=SUB)
            begin[t, rows, :] = begin[t, rows, :] + carried[:, t * LANES:(t + 1) * LANES]

    def chunk_rows(r):
        return pl.ds(pl.multiple_of(r * CHUNK, CHUNK), CHUNK)

    def slot(s):
        return pl.ds(s * WIDTH, WIDTH)

    def g_mate(r):
        return remote(
            gat.at[chunk_rows(r), slot(0)], gat.at[chunk_rows(r), slot(1)],
            gc_s.at[r], gc_r.at[r], mate,
        )

    def g_x(r):
        return remote(
            gat.at[chunk_rows(r), slot(0)], gat.at[chunk_rows(r), slot(2)],
            gx_s.at[r], gx_r.at[r], x_side(0, 0),
        )

    def g_pass(r):
        return remote(
            gat.at[chunk_rows(r), slot(2)], gat.at[chunk_rows(r), slot(3)],
            gf_s.at[r], gf_r.at[r], mate,
        )

    def filter_tile(r, t):
        a = states(decay, t)
        b = states(coef, t)
        direct = skips[t, :, :]

        def step(i, h):
            h = list(h)
            parts = []
            base = r * CHUNK + i * (2 * SUB)
            for u in range(2):
                rows = pl.ds(pl.multiple_of(base + u * SUB, SUB), SUB)
                x = mix[t, rows, :]
                h = [a[m] * h[m] + x for m in range(MODES)]
                terms = [b[m] * h[m] for m in range(MODES)]
                while len(terms) > 1:
                    terms = [terms[j] + terms[j + 1] for j in range(0, len(terms), 2)]
                parts.append(gate[t, rows, :] * (terms[0] + direct * x))
            gat[
                pl.ds(pl.multiple_of(base, 2 * SUB), 2 * SUB),
                pl.ds(pl.multiple_of(t * LANES, LANES), LANES),
            ] = jnp.concatenate(parts, axis=0).astype(BF16)
            return tuple(h)

        h = lax.fori_loop(0, CHUNK // (2 * SUB), step, tuple(states(begin, t)))
        for m in range(MODES):
            begin[t, m * SUB:(m + 1) * SUB, :] = h[m]

    def filter_chunk(r, carry):
        def tile(t, carry):
            filter_tile(r, t)
            return carry

        lax.fori_loop(0, TILES, tile, 0)
        g_x(r).start()
        g_mate(r).start()
        return carry

    lax.fori_loop(0, CHUNKS, filter_chunk, 0)
    pass_on(1, 0)
    pass_on(1, 1)

    def w_ready(d):
        for c in (0, 1):
            for h in (0, 1):
                w_y(d, c, h).wait_recv()

    def product(r, d):
        return jnp.dot(gat[chunk_rows(r), :], wn[d], preferred_element_type=F32)

    def near_product(b):
        rows = pl.ds(pl.multiple_of(b * 256, 256), 256)
        near[rows, :] = jnp.dot(
            gat[rows, 0:2 * WIDTH], wn[0, 0:2 * WIDTH, :], preferred_element_type=F32
        )

    def first_copy(r, device):
        return remote(
            first_out.at[chunk_rows(r)], first_in.at[chunk_rows(r)], f_s.at[r], f_r.at[r], device
        )

    def second_copy(r, side):
        return remote(
            second_out.at[side, chunk_rows(r)], second_in.at[side, chunk_rows(r)],
            s_s.at[side, r], s_r.at[side, r], z_down if side else z_up,
        )

    def first_sum(r):
        g_mate(r).wait_recv()
        g_pass(r).wait_recv()
        first_out[chunk_rows(r), :] = product(r, 2).astype(BF16)

        @pl.when(r < EARLY)
        def _():
            first_copy(r, z_down).start()

        @pl.when(r >= EARLY)
        def _():
            first_copy(r, z_up).start()

    def second_sum(r, side):
        partial = product(r, 3 if side else 1)
        passes = r < EARLY if side else r >= EARLY

        @pl.when(passes)
        def _():
            first_copy(r, z_up).wait_recv()
            second_out[side, chunk_rows(r), :] = (
                partial + first_in[chunk_rows(r), :].astype(F32)
            ).astype(BF16)

        @pl.when(jnp.logical_not(passes))
        def _():
            second_out[side, chunk_rows(r), :] = partial.astype(BF16)

        second_copy(r, side).start()

    def last_sum(r):
        own = near[chunk_rows(r), :] + jnp.dot(
            gat[chunk_rows(r), 2 * WIDTH:4 * WIDTH], wn[0, 2 * WIDTH:4 * WIDTH, :],
            preferred_element_type=F32,
        )
        for side in (0, 1):
            second_copy(r, side).wait_recv()
        own = own + second_in[0, chunk_rows(r), :].astype(F32) + second_in[1, chunk_rows(r), :].astype(F32)
        for t in range(TILES):
            total[t, :, :] = own[:, t * LANES:(t + 1) * LANES]
        piece = CHUNK // SUB
        for n in range(SUB):
            rows = pl.ds(pl.multiple_of(n * BLOCK + r * piece, piece), piece)
            for t in range(TILES):
                out_ref[rows, t * LANES:(t + 1) * LANES] = (
                    total[t, pl.ds(n, piece, stride=SUB), :].astype(BF16)
                )

    def between(first, last, body):
        def step(r, carry):
            body(r)
            return carry

        lax.fori_loop(first, last, step, 0)

    def turn(i, carry):
        for at, c, parts in ((2, 0, (0, 1)), (3, 1, (0,)), (4, 1, (1,))):
            @pl.when(i == at)
            def _(c=c, parts=parts):
                pass_on(3, c, parts)

        g_x(i).wait_recv()
        g_pass(i).start()

        for at, d in ((0, 2), (UP, 1), (DOWN, 3)):
            @pl.when(i == at)
            def _(d=d):
                w_ready(d)

        upward = (i >= UP) & (i <= EARLY)
        between(jnp.where(i == UP, 0, jnp.maximum(i - 1, 0)), jnp.where(upward, i, 0), lambda r: second_sum(r, 0))
        downward = 2 * jnp.maximum(i - DOWN, 0)
        between(downward, jnp.where(i < DOWN, 0, downward + 2), lambda r: second_sum(r, 1))
        first_sum(i)
        return carry

    for d in ORDER:
        w_mate(d).wait_recv()
        w_own(d).wait()
    lax.fori_loop(0, CHUNKS, turn, 0)
    pass_on(0, 0)
    between(2 * (CHUNKS - DOWN), CHUNKS, lambda r: second_sum(r, 1))
    pass_on(0, 1)
    between(0, ROWS // 256, near_product)
    between(EARLY, CHUNKS, lambda r: second_sum(r, 0))
    w_ready(0)
    between(0, CHUNKS, last_sum)

    for d in ORDER:
        for c in (0, 1):
            for h in (0, 1):
                w_x(d, c, h).wait_send()
                w_y(d, c, h).wait_send()
        w_mate(d).wait_send()
    for k in range(1, 8):
        @pl.when(seq + k < 8)
        def _(k=k):
            state_copy(k).wait_send()

    def finish(r, carry):
        g_x(r).wait_send()
        g_mate(r).wait_send()
        g_pass(r).wait_send()
        first_copy(r, z_up).wait_send()
        for side in (0, 1):
            second_copy(r, side).wait_send()
        return carry

    lax.fori_loop(0, CHUNKS, finish, 0)


def local(query_rows, key_rows, value_rows, horizon, residue, skip, w_out):
    dma = pltpu.SemaphoreType.DMA
    hbm = pl.BlockSpec(memory_space=pltpu.HBM)
    vmem = pl.BlockSpec(memory_space=pltpu.VMEM)
    return pl.pallas_call(
        kernel,
        out_shape=pltpu.VMEM((ROWS, WIDTH), BF16),
        in_specs=[hbm] * 7,
        out_specs=vmem,
        scratch_shapes=[
            pltpu.VMEM((3, ROWS, WIDTH), BF16),
            pltpu.VMEM((MODES, WIDTH), F32),
            pltpu.VMEM((MODES, WIDTH), F32),
            pltpu.VMEM((1, WIDTH), F32),
            pltpu.VMEM((TILES, ROWS, LANES), F32),
            pltpu.VMEM((TILES, ROWS, LANES), F32),
            pltpu.VMEM((TILES, MODES * SUB, LANES), F32),
            pltpu.VMEM((TILES, MODES * SUB, LANES), F32),
            pltpu.VMEM((TILES, SUB, LANES), F32),
            pltpu.VMEM((TILES, MODES * SUB, LANES), F32),
            pltpu.VMEM((TILES, MODES * SUB, LANES), F32),
            pltpu.VMEM((8, MODES, WIDTH), F32),
            pltpu.VMEM((ROWS, 4 * WIDTH), BF16),
            pltpu.VMEM((4, 4 * WIDTH, WIDTH), BF16),
            pltpu.VMEM((ROWS, WIDTH), BF16),
            pltpu.VMEM((ROWS, WIDTH), BF16),
            pltpu.VMEM((2, ROWS, WIDTH), BF16),
            pltpu.VMEM((2, ROWS, WIDTH), BF16),
            pltpu.VMEM((ROWS, WIDTH), F32),
            pltpu.VMEM((TILES, CHUNK, LANES), F32),
            dma((3,)), dma((3,)), dma((4,)), dma((4,)), dma((4,)),
            dma((4, 2, 2)), dma((4, 2, 2)), dma((4, 2, 2)), dma((4, 2, 2)),
            dma((8,)), dma((8,)),
            dma((CHUNKS,)), dma((CHUNKS,)), dma((CHUNKS,)), dma((CHUNKS,)),
            dma((CHUNKS,)), dma((CHUNKS,)),
            dma((CHUNKS,)), dma((CHUNKS,)), dma((2, CHUNKS)), dma((2, CHUNKS)),
        ],
        compiler_params=pltpu.CompilerParams(
            collective_id=0, has_side_effects=True, vmem_limit_bytes=60 << 20
        ),
        cost_estimate=pl.CostEstimate(
            flops=2 * ROWS * 16 * WIDTH * WIDTH, bytes_accessed=13 << 20, transcendentals=0
        ),
        name="layer",
    )(query_rows, key_rows, value_rows, horizon, residue, skip.reshape(1, WIDTH), w_out)


def solution(mesh):
    in_specs = (
        P("seq", "chan"),
        P("seq", "chan"),
        P("seq", "chan"),
        P(None, "chan"),
        P(None, "chan"),
        P("chan"),
        P("chan", None),
    )
    out_specs = P("seq", "chan")
    return jax.shard_map(local, mesh=mesh, in_specs=in_specs, out_specs=out_specs, check_vma=False)
```
